128 devices in a mesh: pair: 32 (over y, x, core), rep: 4 (over z).
Axes of the slice: x: 4, y: 4, z: 4, core: 2. Of those that a mesh axis runs over, the one named last changes fastest.
Arguments:
- amplitude: bfloat16 [1600, 16384], P('pair', 'rep'), may hold values from -6 to 6
- tile_mask: int32 [40, 40, 2, 2], replicated, may hold values 0 or 1
- ladder_ints: bfloat16 [16384, 16384], P('rep', 'pair'), may hold values from -0.046875 to 0.046875
- cycle_ints: bfloat16 [128, 40, 5120], P('pair', None, 'rep'), may hold values from -0.078125 to 0.078125
- coulomb: bfloat16 [40, 40, 16384], P('rep', None, 'pair'), may hold values from -6 to 6
- eps_occ: float32 [40], replicated, may hold values from -2 to -0.5
- eps_vir: float32 [128], replicated, may hold values from 0.5 to 3
Outputs:
- amp_new: bfloat16 [40, 40, 16384], P('rep', None, 'pair')
The draws below stay inside these ranges and needn't reach their ends.
All inputs are finite; a program needn't handle non-finite values.
Results may differ from the reference program's by a relative error of at most 0.001.
Values may be sent and summed in bfloat16 or wider, within the bound.
A program may use at most 128 MiB of HBM per device.

```python
import jax
import jax.numpy as jnp

NO = 40
NV = 128
TILE = 64
NVT = 2


def with_ends(values, rng, least, high):
    longest = values.shape.index(max(values.shape))
    spots = []
    for shift in (0, 1):
        where = [jax.random.randint(jax.random.fold_in(rng, axis), (), 0, length) for axis, length in enumerate(values.shape)]
        where[longest] = (where[longest] + shift) % values.shape[longest]
        spots.append(tuple(where))
    return values.at[spots[0]].set(least).at[spots[1]].set(high)


def steps_of(own_key, dims, split, low, high):
    factor_of = 1.0
    for axis_at, parts in split:
        heights = jax.random.uniform(jax.random.fold_in(jax.random.fold_in(own_key, 6), axis_at), (parts,), jnp.float32, low / len(split), high / len(split))
        factor_of = factor_of * jnp.repeat(jnp.exp(heights), dims[axis_at] // parts).reshape((-1,) + (1,) * (len(dims) - 1 - axis_at))
    return factor_of


def normal_values(stream_key, shape, deviation, reach, split=(), kind=jnp.bfloat16):
    loudness = steps_of(stream_key, shape, split, -0.22, 0.18) if split else 1.0
    result = jax.random.normal(stream_key, shape, jnp.float32) * deviation * loudness
    return jnp.minimum(jnp.maximum(result, -reach), reach).astype(kind)


def setup_inputs(seed: int = 0) -> dict:
    key_list = jax.random.split(jax.random.key(seed), 8)
    amplitude = normal_values(key_list[0], (NO * NO, NV * NV), 1.0, 6.0, ((0, 32), (1, 4)))
    tile_mask = with_ends((jax.random.randint(key_list[1], (NO, NO, NVT, NVT), 0, 4) < 3).astype(jnp.int32), jax.random.fold_in(key_list[1], 1), 0, 1)
    ladder_ints = normal_values(key_list[2], (NV * NV, NV * NV), (NV * NV) ** -0.5, 0.046875, ((0, 4), (1, 32)))
    cycle_ints = normal_values(key_list[3], (NV, NO, NV * NO), (NO * NV) ** -0.5, 0.078125, ((0, 32), (2, 4)))
    coulomb = normal_values(key_list[4], (NO, NO, NV * NV), 1.0, 6.0, ((0, 4), (2, 32)))
    eps_occ = jnp.clip(jax.random.uniform(key_list[5], (NO,), jnp.float32, -2.0, -0.5), -2.0, -0.5)
    eps_vir = jnp.clip(jax.random.uniform(key_list[6], (NV,), jnp.float32, 0.5, 3.0), 0.5, 3.0)
    return {"amplitude": amplitude, "tile_mask": tile_mask, "ladder_ints": ladder_ints, "cycle_ints": cycle_ints, "coulomb": coulomb, "eps_occ": eps_occ, "eps_vir": eps_vir}


def reference(amplitude, tile_mask, ladder_ints, cycle_ints, coulomb, eps_occ, eps_vir):
    expanded = jnp.repeat(jnp.repeat(tile_mask, TILE, axis=2), TILE, axis=3)
    screened = amplitude * expanded.reshape(NO * NO, NV * NV).astype(amplitude.dtype)
    ladder = jnp.dot(screened, ladder_ints, preferred_element_type=jnp.float32).reshape(NO, NO, NV, NV)
    right = jnp.transpose(screened.reshape(NO, NO, NV, NV), (2, 0, 1, 3)).reshape(NV * NO, NO * NV)
    cycle = jnp.dot(cycle_ints.reshape(NV * NO, NV * NO), right,
                   preferred_element_type=jnp.float32).reshape(NV, NO, NO, NV)
    residual = coulomb.astype(jnp.float32).reshape(NO, NO, NV, NV) + ladder
    residual = residual + jnp.transpose(cycle, (1, 2, 0, 3)) + jnp.transpose(cycle, (2, 1, 3, 0))
    denom = (eps_vir[None, None, :, None] + eps_vir[None, None, None, :]
             - eps_occ[:, None, None, None] - eps_occ[None, :, None, None])
    return (residual / denom).astype(jnp.bfloat16).reshape(NO, NO, NV * NV)
```

```python
import jax
import jax.numpy as jnp
from jax import lax
from jax.experimental import pallas as pl
from jax.experimental.pallas import tpu as pltpu
from jax.sharding import PartitionSpec as P

NG = 5
NM = 8
NK = 40
ROWS = 10
NC = 32
F32 = jnp.float32
BF16 = jnp.bfloat16
MESH = pl.DeviceIdType.MESH


def kernel(
    amp_ref, mask_ref, v_hbm, w_ref, lbar_ref, xbar_ref,
    s, v, tmp, s2, lad, cyc, lad_far, cyc_far, lad_in, cyc_in,
    v_sem, send_s, recv_f, recv_g, recv_b, send_r, recv_far, recv_in,
):
    p = lax.axis_index("pair")
    r = lax.axis_index("rep")
    h = p % 2
    x = (p // 2) % 4
    y = p // 8
    f = x + h * (y - x)
    gg = y + h * (x - y)
    sf = 1 + 3 * h
    sg = 4 - 3 * h

    def blk(df, dg):
        return 2 * (((f + df) % 4) * sf + ((gg + dg) % 4) * sg) + h

    sib = p + 1 - 2 * h
    fp, fm, gp, gm = blk(1, 0), blk(3, 0), blk(0, 1), blk(0, 3)
    up, down, far = (r + 1) % 4, (r + 3) % 4, (r + 2) % 4

    pltpu.make_async_copy(v_hbm, v, v_sem).start()

    barrier = pltpu.get_barrier_semaphore()
    for q in (fp, fm, gp, gm, sib):
        pl.semaphore_signal(barrier, inc=1, device_id=(q, r), device_id_type=MESH)
    for q in (up, down):
        pl.semaphore_signal(barrier, inc=1, device_id=(p, q), device_id_type=MESH)

    for c in range(NC):
        piece = amp_ref[:, c * 128 : (c + 1) * 128].astype(F32) * mask_ref[...]
        tmp[pl.ds(c, 50, stride=NC), :] = piece
    for n in range(50):
        s[n % NG, p, n // NG] = tmp[n * NC : (n + 1) * NC, :].astype(BF16)

    pl.semaphore_wait(barrier, 7)

    def send(src, dst, ssem, rsem, dev):
        pltpu.make_async_remote_copy(
            src_ref=src, dst_ref=dst, send_sem=ssem, recv_sem=rsem, device_id=dev, device_id_type=MESH
        ).start()

    def wait(ref, sem):
        pltpu.make_async_copy(ref, ref, sem).wait()

    def whole(g, b, sem, to):
        send(s.at[g, b], s.at[g, b], send_s.at[g], sem, (to, r))

    def half(g, b, at, sem, to):
        send(s.at[g, b, pl.ds(at, 5)], s.at[g, b, pl.ds(at, 5)], send_s.at[g], sem, (to, r))

    offs = (0, 3, 1, 2)

    def start_own(g):
        whole(g, p, recv_f.at[g, 0], fp)
        whole(g, p, recv_f.at[g, 1], fm)
        start_g(g, 0)

    def start_g(g, col):
        b = blk(offs[col], 0)
        whole(g, b, recv_g.at[g, col, 0], gp)
        whole(g, b, recv_g.at[g, col, 1], gm)
        whole(g, b, recv_b.at[g, col], sib)

    def pass_f(g):
        wait(s.at[g, 0], recv_f.at[g, 0])
        half(g, fm, 0, recv_f.at[g, 2], fp)
        start_g(g, 1)
        wait(s.at[g, 0], recv_f.at[g, 1])
        half(g, fp, 5, recv_f.at[g, 2], fm)
        start_g(g, 2)

    def last_f(g):
        wait(s.at[g, 0], recv_f.at[g, 2])
        start_g(g, 3)

    def pass_g(g, col):
        below, above = blk(offs[col], 3), blk(offs[col], 1)
        wait(s.at[g, 0], recv_g.at[g, col, 0])
        half(g, below, 0, recv_g.at[g, col, 2], gp)
        whole(g, below, recv_b.at[g, col], sib)
        wait(s.at[g, 0], recv_g.at[g, col, 1])
        half(g, above, 5, recv_g.at[g, col, 2], gm)
        whole(g, above, recv_b.at[g, col], sib)

    def last_g(g, col):
        wait(s.at[g, 0], recv_g.at[g, col, 2])
        whole(g, blk(offs[col], 2), recv_b.at[g, col], sib)

    def quarter(g, n):
        if n % 2 == 0:
            c0 = 16 * (n // 2)

            def widen(b, _):
                for u in range(ROWS):
                    tmp[pl.ds(pl.multiple_of((b * ROWS + u) * 16, 16), 16), :] = s[g, b, u, c0 : c0 + 16, :].astype(F32)
                return 0

            lax.fori_loop(0, 32, widen, 0)
        for c in range(8):
            s2[:, c * 128 : (c + 1) * 128] = tmp[pl.ds(8 * (n % 2) + c, 320, stride=16), :].astype(BF16)
        part = jnp.dot(s2[...], v[n * 1024 : (n + 1) * 1024, :], preferred_element_type=F32)
        for a in range(4):
            if n == 0:
                lad[g, a] = part[:, a * 128 : (a + 1) * 128]
            else:
                lad[g, a] += part[:, a * 128 : (a + 1) * 128]
        rows = []
        for k in range(NK):
            b0, u0 = divmod(NM * k + 2 * n, ROWS)
            b1, u1 = divmod(NM * k + 2 * n + 1, ROWS)
            rows.append(jnp.concatenate([s[g, b0, u0], s[g, b1, u1]], axis=1))
        got = jnp.dot(w_ref[...], jnp.concatenate(rows, axis=0), preferred_element_type=F32)
        cyc[g, n] = got
        for m in range(2):
            for a in range(4):
                lad[g, a, pl.ds(2 * n + m, NK, stride=NM), :] += got[
                    a * NK : (a + 1) * NK, m * 128 : (m + 1) * 128
                ]

    def rows_of(t):
        return pl.ds(pl.multiple_of(t * 80, 80), 80)

    def reduce_1(g):
        send(lad.at[g, :, rows_of(far)], lad_far.at[g], send_r.at[g, 0], recv_far.at[g, 0], (p, up))
        send(cyc.at[g, far], cyc_far.at[g], send_r.at[g, 1], recv_far.at[g, 1], (p, down))
        send(cyc.at[g, up], cyc_in.at[g, 0], send_r.at[g, 2], recv_in.at[g, 0], (p, up))
        send(lad.at[g, :, rows_of(down)], lad_in.at[g, 1], send_r.at[g, 3], recv_in.at[g, 1], (p, down))

    def reduce_2(g):
        wait(lad_far.at[g], recv_far.at[g, 0])
        lad[g, :, rows_of(up), :] += lad_far[g]
        send(lad.at[g, :, rows_of(up)], lad_in.at[g, 0], send_r.at[g, 4], recv_in.at[g, 2], (p, up))
        wait(cyc_far.at[g], recv_far.at[g, 1])
        cyc[g, down] += cyc_far[g]
        send(cyc.at[g, down], cyc_in.at[g, 1], send_r.at[g, 5], recv_in.at[g, 3], (p, down))

    def reduce_3(g):
        wait(cyc_in.at[g, 0], recv_in.at[g, 0])
        wait(lad_in.at[g, 1], recv_in.at[g, 1])
        wait(lad_in.at[g, 0], recv_in.at[g, 2])
        wait(cyc_in.at[g, 1], recv_in.at[g, 3])
        xbar_ref[g] = cyc[g, r] + cyc_in[g, 0] + cyc_in[g, 1]
        total = lad[g, :, rows_of(r), :] + lad_in[g, 0] + lad_in[g, 1]
        for i in range(10):
            for a in range(4):
                lbar_ref[a, pl.ds(i * NK + g, NM, stride=NG), :] = total[a, i * NM : (i + 1) * NM, :]

    start_own(0)
    wait(v, v_sem)

    def step(it, _):
        on, back = it < NG, it >= 1
        done = it - 1
        pl.when(on)(lambda: pass_f(it))
        pl.when(back)(lambda: quarter(done, 0))

        @pl.when(on)
        def _():
            pass_g(it, 0)
            last_f(it)

        pl.when(back)(lambda: quarter(done, 1))
        pl.when(it >= 2)(lambda: reduce_2(it - 2))

        @pl.when(on)
        def _():
            pass_g(it, 1)
            pass_g(it, 2)

        pl.when(it + 1 < NG)(lambda: start_own(it + 1))
        pl.when(back)(lambda: quarter(done, 2))

        @pl.when(on)
        def _():
            last_g(it, 0)
            last_g(it, 1)
            pass_g(it, 3)

        @pl.when(back)
        def _():
            quarter(done, 3)
            reduce_1(done)

        @pl.when(on)
        def _():
            last_g(it, 2)
            last_g(it, 3)
            for col in range(4):
                wait(s.at[it, pl.ds(0, 4)], recv_b.at[it, col])

        return 0

    lax.fori_loop(0, NG + 1, step, 0)
    reduce_2(NG - 1)

    def finish(g, _):
        reduce_3(g)
        wait(s.at[g, pl.ds(0, 31)], send_s.at[g])
        for n in range(6):
            if n in (0, 3, 4):
                wait(lad_far.at[g], send_r.at[g, n])
            else:
                wait(cyc_far.at[g], send_r.at[g, n])
        return 0

    lax.fori_loop(0, NG, finish, 0)


def fused(amp, mask, v, w):
    vmem = pl.BlockSpec(memory_space=pltpu.VMEM)
    dma = pltpu.SemaphoreType.DMA
    return pl.pallas_call(
        kernel,
        out_shape=(
            jax.ShapeDtypeStruct((4, 400, 128), F32),
            jax.ShapeDtypeStruct((NG, 160, 256), F32),
        ),
        in_specs=[vmem, vmem, pl.BlockSpec(memory_space=pl.ANY), vmem],
        out_specs=(vmem, vmem),
        scratch_shapes=[
            pltpu.VMEM((NG, 32, ROWS, NC, 128), BF16),
            pltpu.VMEM((4096, 512), BF16),
            pltpu.VMEM((320 * 16, 128), F32),
            pltpu.VMEM((320, 1024), BF16),
            pltpu.VMEM((NG, 4, 320, 128), F32),
            pltpu.VMEM((NG, 4, 160, 256), F32),
            pltpu.VMEM((NG, 4, 80, 128), F32),
            pltpu.VMEM((NG, 160, 256), F32),
            pltpu.VMEM((NG, 2, 4, 80, 128), F32),
            pltpu.VMEM((NG, 2, 160, 256), F32),
            dma,
            dma((NG,)),
            dma((NG, 3)),
            dma((NG, 4, 3)),
            dma((NG, 4)),
            dma((NG, 6)),
            dma((NG, 2)),
            dma((NG, 4)),
        ],
        compiler_params=pltpu.CompilerParams(
            collective_id=0, has_side_effects=True, vmem_limit_bytes=60 * 1024 * 1024
        ),
    )(amp, mask, v, w)


def shards(amplitude, tile_mask, ladder_ints, cycle_ints, coulomb, eps_occ, eps_vir):
    pair_at = lax.axis_index("pair")
    rep_at = lax.axis_index("rep")
    rows = lax.dynamic_slice(tile_mask.reshape(1600, 2, 2), (pair_at * 50, rep_at // 2, 0), (50, 1, 2))
    mask = jnp.repeat(rows.reshape(50, 2).astype(F32), 64, axis=1)
    w = cycle_ints.reshape(160, NC, NK).swapaxes(1, 2).reshape(160, NK * NC)
    lbar, xbar = fused(amplitude, mask, ladder_ints, w)
    swapped = lax.all_to_all(xbar.reshape(NG, 4, 40, 2, 32, 4), "pair", split_axis=4, concat_axis=4, tiled=True)
    mirror = jnp.transpose(swapped, (3, 0, 2, 5, 4, 1)).reshape(10, 40, 512)
    occ_mine = lax.dynamic_slice_in_dim(eps_occ, rep_at * 10, 10, 0)
    vir_first = lax.dynamic_slice_in_dim(eps_vir, pair_at * 4, 4, 0)
    vir_pairs = (vir_first[:, None] + eps_vir[None, :]).reshape(512)
    denom = vir_pairs[None, None, :] - occ_mine[:, None, None] - eps_occ[None, :, None]
    residual = coulomb.astype(F32) + lbar.swapaxes(0, 1).reshape(10, 40, 512) + mirror
    return (residual / denom).astype(BF16)


def solution(mesh):
    placed = (
        P("pair", "rep"),
        P(),
        P("rep", "pair"),
        P("pair", None, "rep"),
        P("rep", None, "pair"),
        P(),
        P(),
    )
    return jax.shard_map(
        shards, mesh=mesh, in_specs=placed, out_specs=P("rep", None, "pair"), check_vma=False
    )
```

```python
import jax
import jax.numpy as jnp
from jax import lax
from jax.experimental import pallas as pl
from jax.experimental.pallas import tpu as pltpu
from jax.sharding import PartitionSpec as P

NG = 5
NM = 8
NK = 40
STEPS = 32512.0
ROWS = 10
NC = 32
F32 = jnp.float32
BF16 = jnp.bfloat16
MESH = pl.DeviceIdType.MESH


def encode(dst, val):
    size = jnp.maximum(jnp.max(jnp.abs(val), axis=0, keepdims=True), 1e-30)
    log = jnp.ceil(jnp.log(size) * 128.0)
    dst[0:320] = jnp.round(val * (jnp.exp(log * (-1 / 128)) * STEPS)).astype(jnp.int32).astype(jnp.int16)
    dst[320:336] = jnp.broadcast_to(log, (16, 128)).astype(jnp.int32).astype(jnp.int16)


def decode(src):
    log = src[320:336].astype(jnp.int32).astype(F32)[0:1]
    return src[0:320].astype(jnp.int32).astype(F32) * (jnp.exp(log * (1 / 128)) * (1 / STEPS))


def kernel(
    amp_ref, mask_ref, v_hbm, w_ref, coul_ref, occ_ref, vir_ref, occ_smem, vir_smem, out_ref,
    s, v, wnat, wp, tmp, s2, lad, cyc, red_out, red_in, msg, z, msg_out, msg_in, fin, mir,
    v_sem, send_s, recv_f, recv_g, recv_b, send_r, recv_r, send_m, recv_m,
):
    p = lax.axis_index("pair")
    r = lax.axis_index("rep")
    h = p % 2
    x = (p // 2) % 4
    y = p // 8
    f = x + h * (y - x)
    gg = y + h * (x - y)
    sf = 1 + 3 * h
    sg = 4 - 3 * h

    def blk(df, dg):
        return 2 * (((f + df) % 4) * sf + ((gg + dg) % 4) * sg) + h

    sib = p + 1 - 2 * h
    fp, fm, gp, gm = blk(1, 0), blk(3, 0), blk(0, 1), blk(0, 3)
    up, down, far = (r + 1) % 4, (r + 3) % 4, (r + 2) % 4

    pltpu.make_async_copy(v_hbm, v, v_sem).start()

    barrier = pltpu.get_barrier_semaphore()

    @pl.loop(1, 32)
    def _(n):
        pl.semaphore_signal(barrier, inc=1, device_id=((p + n) % 32, r), device_id_type=MESH)

    for q in (up, down):
        pl.semaphore_signal(barrier, inc=1, device_id=(p, q), device_id_type=MESH)

    for c in range(NC):
        piece = amp_ref[:, c * 128 : (c + 1) * 128].astype(F32) * mask_ref[...]
        tmp[pl.ds(c, 50, stride=NC), :] = piece
    for n in range(50):
        s[n % NG, p, n // NG] = tmp[n * NC : (n + 1) * NC, :].astype(BF16)

    pl.semaphore_wait(barrier, 33)

    def send(src, dst, ssem, rsem, dev):
        pltpu.make_async_remote_copy(
            src_ref=src, dst_ref=dst, send_sem=ssem, recv_sem=rsem, device_id=dev, device_id_type=MESH
        ).start()

    def wait(ref, sem):
        pltpu.make_async_copy(ref, ref, sem).wait()

    def whole(g, b, sem, to):
        send(s.at[g, b], s.at[g, b], send_s.at[g], sem, (to, r))

    def half(g, b, at, sem, to):
        send(s.at[g, b, pl.ds(at, 5)], s.at[g, b, pl.ds(at, 5)], send_s.at[g], sem, (to, r))

    offs = (0, 3, 1, 2)

    def start_f(g):
        whole(g, p, recv_f.at[g, 0], fp)
        whole(g, p, recv_f.at[g, 1], fm)

    def start_g(g, col):
        b = blk(offs[col], 0)
        whole(g, b, recv_g.at[g, col, 0], gp)
        whole(g, b, recv_g.at[g, col, 1], gm)
        whole(g, b, recv_b.at[g, col], sib)

    def pass_f(g):
        wait(s.at[g, 0], recv_f.at[g, 0])
        half(g, fm, 0, recv_f.at[g, 2], fp)
        wait(s.at[g, 0], recv_f.at[g, 1])
        half(g, fp, 5, recv_f.at[g, 2], fm)

    def last_f(g):
        wait(s.at[g, 0], recv_f.at[g, 2])

    def pass_g(g, col):
        below, above = blk(offs[col], 3), blk(offs[col], 1)
        wait(s.at[g, 0], recv_g.at[g, col, 0])
        half(g, below, 0, recv_g.at[g, col, 2], gp)
        whole(g, below, recv_b.at[g, col], sib)
        wait(s.at[g, 0], recv_g.at[g, col, 1])
        half(g, above, 5, recv_g.at[g, col, 2], gm)
        whole(g, above, recv_b.at[g, col], sib)

    def last_g(g, col):
        wait(s.at[g, 0], recv_g.at[g, col, 2])
        whole(g, blk(offs[col], 2), recv_b.at[g, col], sib)

    def sort_w():
        for a in range(4):
            wnat[a * NK : (a + 1) * NK, :] = w_ref[a].astype(F32)
        total = jnp.zeros((160, 1280), F32)
        for n in range(5):
            row = n * 256 + lax.broadcasted_iota(jnp.int32, (256, 1280), 0)
            col = lax.broadcasted_iota(jnp.int32, (256, 1280), 1)
            perm = (row == (col & 31) * NK + (col >> 5)).astype(F32).astype(BF16)
            total += jnp.dot(wnat[:, n * 256 : (n + 1) * 256].astype(BF16), perm, preferred_element_type=F32)
        wp[...] = total.astype(BF16)

    def quarter(g, n):
        if n % 2 == 0:
            c0 = 16 * (n // 2)

            def widen(b, _):
                for u in range(ROWS):
                    tmp[pl.ds(pl.multiple_of((b * ROWS + u) * 16, 16), 16), :] = s[g, b, u, c0 : c0 + 16, :].astype(F32)
                return 0

            lax.fori_loop(0, 32, widen, 0)
        for c in range(8):
            s2[:, c * 128 : (c + 1) * 128] = tmp[pl.ds(8 * (n % 2) + c, 320, stride=16), :].astype(BF16)
        part = jnp.dot(s2[...], v[n * 1024 : (n + 1) * 1024, :], preferred_element_type=F32)
        for a in range(4):
            if n == 0:
                lad[g, a] = part[:, a * 128 : (a + 1) * 128]
            else:
                lad[g, a] += part[:, a * 128 : (a + 1) * 128]
        rows = []
        for k in range(NK):
            b0, u0 = divmod(NM * k + 2 * n, ROWS)
            b1, u1 = divmod(NM * k + 2 * n + 1, ROWS)
            rows.append(jnp.concatenate([s[g, b0, u0], s[g, b1, u1]], axis=1))
        got = jnp.dot(wp[...], jnp.concatenate(rows, axis=0), preferred_element_type=F32)
        cyc[g, n, 0] = got[:, 0:128]
        cyc[g, n, 1] = got[:, 128:256]
        for m in range(2):
            for a in range(4):
                lad[g, a, pl.ds(2 * n + m, NK, stride=NM), :] += got[
                    a * NK : (a + 1) * NK, m * 128 : (m + 1) * 128
                ]

    def rows_of(t):
        return pl.ds(pl.multiple_of(t * 80, 80), 80)

    def lad_of(g, t):
        return lad[g, :, rows_of(t), :].reshape(320, 128)

    def cyc_of(g, t):
        return cyc[g, t].reshape(320, 128)

    def ship(g, n, val, to):
        encode(red_out.at[g, n], val)
        send(red_out.at[g, n], red_in.at[g, n], send_r.at[g], recv_r.at[g, n], (p, to))

    def take(g, n):
        wait(red_in.at[g, n], recv_r.at[g, n])
        return decode(red_in.at[g, n])

    def reduce_1(g):
        ship(g, 0, lad_of(g, far), up)
        ship(g, 2, cyc_of(g, far), down)
        ship(g, 1, cyc_of(g, up), up)
        ship(g, 3, lad_of(g, down), down)

    def reduce_2(g):
        ship(g, 4, lad_of(g, up) + take(g, 0), up)
        ship(g, 5, cyc_of(g, down) + take(g, 2), down)

    def reduce_3(g):
        whole_cyc = (cyc_of(g, r) + take(g, 1) + take(g, 5)).reshape(2, 160, 128)
        for b in range(4):
            val = whole_cyc[:, b * NK : (b + 1) * NK, :].reshape(80, 128)
            size = jnp.maximum(jnp.max(jnp.abs(val), axis=0, keepdims=True), 1e-30)
            log = jnp.ceil(jnp.log(size) * 128.0)
            code = jnp.round(val * (jnp.exp(log * (-1 / 128)) * STEPS))
            msg[pl.ds(b, 128, stride=4), :] = jnp.concatenate([code, jnp.broadcast_to(log, (48, 128))], axis=0).T
        msg_out[g] = msg[...].astype(jnp.int32).astype(jnp.int16).reshape(32, 16, 128)
        msg_in[g, p] = msg_out[g, p]
        total = (lad_of(g, r) + take(g, 3) + take(g, 4)).reshape(4, 80, 128)
        for i in range(10):
            for a in range(4):
                fin[a, pl.ds(i * NK + g, NM, stride=NG), :] = total[a, i * NM : (i + 1) * NM, :]

    batches = ((0, NG - 1), (NG - 1, 1))

    def exchange(n):
        at = pl.ds(*batches[n])

        @pl.loop(1, 32)
        def _(d):
            to = (p + d) % 32
            send(msg_out.at[at, to], msg_in.at[at, p], send_m.at[n], recv_m.at[n], (to, r))

    def exchanged(n):
        part = msg_in.at[pl.ds(*batches[n]), pl.ds(0, 31)]
        wait(part, recv_m.at[n])

    def mirror(g):
        msg[...] = msg_in[g].reshape(512, 128).astype(jnp.int32).astype(F32)
        for a in range(4):
            for b in range(4):
                z[a, pl.ds(b, 32, stride=4), :] = msg[pl.ds(a * 4 + b, 32, stride=16), :]
        for a in range(4):
            turned = z[a].T
            val = turned[0:80] * (jnp.exp(turned[80:81] * (1 / 128)) * (1 / STEPS))
            for m in range(2):
                mir[a, pl.ds(pl.multiple_of((NG * m + g) * NK, 8), NK), :] = val[m * NK : (m + 1) * NK]

    start_f(0)

    def step(it, _):
        new, old, done = it, it - 1, it - 2
        is_new, is_old, is_done = it < NG, (it >= 1) & (it <= NG), it >= 2

        @pl.when(is_new)
        def _():
            start_g(new, 0)

        @pl.when(is_old)
        def _():
            pass_g(old, 2)
            last_g(old, 0)

        @pl.when(is_done)
        def _():
            for col in range(4):
                wait(s.at[done, pl.ds(0, 4)], recv_b.at[done, col])
            quarter(done, 0)

        @pl.when(is_new)
        def _():
            pass_f(new)
            start_g(new, 1)

        @pl.when(it == 1)
        def _():
            sort_w()
            wait(v, v_sem)

        @pl.when(is_old)
        def _():
            pass_g(old, 3)
            last_g(old, 1)

        pl.when(is_done)(lambda: quarter(done, 1))
        pl.when(it >= 3)(lambda: reduce_2(it - 3))

        @pl.when(is_new)
        def _():
            pass_g(new, 0)
            start_g(new, 2)

        pl.when(is_old)(lambda: last_g(old, 2))
        pl.when(is_done)(lambda: quarter(done, 2))
        pl.when(it + 1 < NG)(lambda: start_f(it + 1))

        @pl.when(is_new)
        def _():
            last_f(new)
            start_g(new, 3)
            pass_g(new, 1)

        pl.when(is_old)(lambda: last_g(old, 3))

        @pl.when(is_done)
        def _():
            quarter(done, 3)
            reduce_1(done)

        pl.when(it >= 3)(lambda: reduce_3(it - 3))
        return 0

    lax.fori_loop(0, NG + 2, step, 0)
    exchange(0)
    reduce_2(NG - 1)
    reduce_3(NG - 1)
    exchange(1)
    exchanged(0)

    @pl.loop(0, NG - 1)
    def _(g):
        mirror(g)

    exchanged(1)
    mirror(NG - 1)

    @pl.loop(0, 10)
    def _(i):
        rows = pl.ds(pl.multiple_of(i * NK, 8), NK)
        for a in range(4):
            lanes = slice(a * 128, (a + 1) * 128)
            residual = coul_ref[i, :, lanes].astype(F32) + fin[a, rows, :] + mir[a, rows, :]
            denom = (vir_smem[p * 4 + a] + vir_ref[...]) - occ_smem[r * 10 + i] - occ_ref[...]
            out_ref[i, :, lanes] = (residual / denom).astype(BF16)

    for g in range(NG):
        wait(s.at[g, pl.ds(0, 31)], send_s.at[g])
        wait(red_out.at[g], send_r.at[g])
    for n in range(2):
        wait(msg_out.at[pl.ds(*batches[n]), pl.ds(0, 31)], send_m.at[n])


def fused(amp, mask, v, w, coulomb, eps_occ, eps_vir):
    vmem = pl.BlockSpec(memory_space=pltpu.VMEM)
    smem = pl.BlockSpec(memory_space=pltpu.SMEM)
    dma = pltpu.SemaphoreType.DMA
    return pl.pallas_call(
        kernel,
        out_shape=jax.ShapeDtypeStruct((10, NK, 512), BF16),
        in_specs=[vmem, vmem, pl.BlockSpec(memory_space=pl.ANY), vmem, vmem, vmem, vmem, smem, smem],
        out_specs=vmem,
        scratch_shapes=[
            pltpu.VMEM((NG, 32, ROWS, NC, 128), BF16),
            pltpu.VMEM((4096, 512), BF16),
            pltpu.VMEM((160, 1280), F32),
            pltpu.VMEM((160, 1280), BF16),
            pltpu.VMEM((320 * 16, 128), F32),
            pltpu.VMEM((320, 1024), BF16),
            pltpu.VMEM((NG, 4, 320, 128), F32),
            pltpu.VMEM((NG, 4, 2, 160, 128), F32),
            pltpu.VMEM((NG, 6, 336, 128), jnp.int16),
            pltpu.VMEM((NG, 6, 336, 128), jnp.int16),
            pltpu.VMEM((512, 128), F32),
            pltpu.VMEM((4, 128, 128), F32),
            pltpu.VMEM((NG, 32, 16, 128), jnp.int16),
            pltpu.VMEM((NG, 32, 16, 128), jnp.int16),
            pltpu.VMEM((4, 400, 128), F32),
            pltpu.VMEM((4, 400, 128), F32),
            dma,
            dma((NG,)),
            dma((NG, 3)),
            dma((NG, 4, 3)),
            dma((NG, 4)),
            dma((NG,)),
            dma((NG, 6)),
            dma((2,)),
            dma((2,)),
        ],
        compiler_params=pltpu.CompilerParams(
            collective_id=0, has_side_effects=True, vmem_limit_bytes=60 * 1024 * 1024
        ),
    )(amp, mask, v, w, coulomb, eps_occ.reshape(NK, 1), eps_vir.reshape(1, 128), eps_occ, eps_vir)


def shards(amplitude, tile_mask, ladder_ints, cycle_ints, coulomb, eps_occ, eps_vir):
    pair_at = lax.axis_index("pair")
    rep_at = lax.axis_index("rep")
    rows = lax.dynamic_slice(tile_mask.reshape(1600, 2, 2), (pair_at * 50, rep_at // 2, 0), (50, 1, 2))
    mask = jnp.repeat(rows.reshape(50, 2).astype(F32), 64, axis=1)
    return fused(amplitude, mask, ladder_ints, cycle_ints, coulomb, eps_occ, eps_vir)


def solution(mesh):
    placed = (
        P("pair", "rep"),
        P(),
        P("rep", "pair"),
        P("pair", None, "rep"),
        P("rep", None, "pair"),
        P(),
        P(),
    )
    return jax.shard_map(
        shards, mesh=mesh, in_specs=placed, out_specs=P("rep", None, "pair"), check_vma=False
    )
```

```python
import jax
import jax.numpy as jnp
from jax import lax
from jax.experimental import pallas as pl
from jax.experimental.pallas import tpu as pltpu
from jax.sharding import PartitionSpec as P

NG = 5
NM = 8
NK = 40
STEPS = 32512.0
ROWS = 10
NC = 32
F32 = jnp.float32
BF16 = jnp.bfloat16
MESH = pl.DeviceIdType.MESH


def encode(dst, val):
    size = jnp.maximum(jnp.max(jnp.abs(val), axis=0, keepdims=True), 1e-30)
    log = jnp.ceil(jnp.log(size) * 128.0)
    dst[0:320] = jnp.round(val * (jnp.exp(log * (-1 / 128)) * STEPS)).astype(jnp.int32).astype(jnp.int16)
    dst[320:336] = jnp.broadcast_to(log, (16, 128)).astype(jnp.int32).astype(jnp.int16)


def decode(src):
    log = src[320:336].astype(jnp.int32).astype(F32)[0:1]
    return src[0:320].astype(jnp.int32).astype(F32) * (jnp.exp(log * (1 / 128)) * (1 / STEPS))


def kernel(
    amp_ref, mask_ref, v_hbm, w_ref, coul_ref, occ_ref, vir_ref, occ_smem, vir_smem, out_ref,
    s, v, wnat, wp, tmp, s2, lad, cyc, red_out, red_in, msg, z, msg_out, msg_in, fin, mir,
    v_sem, send_s, recv_f, recv_g, recv_b, send_r, recv_r, send_m, recv_m,
):
    p = lax.axis_index("pair")
    r = lax.axis_index("rep")
    h = p % 2
    x = (p // 2) % 4
    y = p // 8
    f = x + h * (y - x)
    gg = y + h * (x - y)
    sf = 1 + 3 * h
    sg = 4 - 3 * h

    def dev(df, dg):
        return 2 * (((f + df) % 4) * sf + ((gg + dg) % 4) * sg) + h

    sib = p + 1 - 2 * h
    fp, fm, gp, gm = dev(1, 0), dev(3, 0), dev(0, 1), dev(0, 3)
    up, down, far = (r + 1) % 4, (r + 3) % 4, (r + 2) % 4

    pltpu.make_async_copy(v_hbm, v, v_sem).start()

    barrier = pltpu.get_barrier_semaphore()

    @pl.loop(1, 32)
    def _(n):
        pl.semaphore_signal(barrier, inc=1, device_id=((p + n) % 32, r), device_id_type=MESH)

    for q in (up, down):
        pl.semaphore_signal(barrier, inc=1, device_id=(p, q), device_id_type=MESH)

    for c in range(NC):
        piece = amp_ref[:, c * 128 : (c + 1) * 128].astype(F32) * mask_ref[...]
        tmp[pl.ds(c, 50, stride=NC), :] = piece

    def own(g):
        for u in range(ROWS):
            n = u * NG + g
            s[g, h, f, gg, u] = tmp[n * NC : (n + 1) * NC, :].astype(BF16)

    own(0)
    pl.semaphore_wait(barrier, 33)

    def send(src, dst, ssem, rsem, dev):
        pltpu.make_async_remote_copy(
            src_ref=src, dst_ref=dst, send_sem=ssem, recv_sem=rsem, device_id=dev, device_id_type=MESH
        ).start()

    def wait(ref, sem):
        pltpu.make_async_copy(ref, ref, sem).wait()

    def ship_s(g, at, sem, to):
        send(s.at[(g, h) + at], s.at[(g, h) + at], send_s.at[g], sem, (to, r))

    def start_f(g):
        ship_s(g, (f, gg), recv_f.at[g, 0], fp)
        ship_s(g, (f, gg), recv_f.at[g, 1], fm)

    def pass_f(g):
        wait(s.at[g, 0, 0, 0], recv_f.at[g, 0])
        ship_s(g, ((f + 3) % 4, gg, pl.ds(0, 5)), recv_f.at[g, 2], fp)
        wait(s.at[g, 0, 0, 0], recv_f.at[g, 1])
        ship_s(g, ((f + 1) % 4, gg, pl.ds(5, 5)), recv_f.at[g, 2], fm)

    def last_f(g):
        wait(s.at[g, 0, 0, 0], recv_f.at[g, 2])

    def col(n):
        return (f + (0, 3, 1, 2)[n]) % 4

    def start_g(g, n):
        ship_s(g, (col(n), gg), recv_g.at[g, n, 0], gp)
        ship_s(g, (col(n), gg), recv_g.at[g, n, 1], gm)

    def pass_g(g, n):
        wait(s.at[g, 0, 0, 0], recv_g.at[g, n, 0])
        ship_s(g, (col(n), (gg + 3) % 4, pl.ds(0, 5)), recv_g.at[g, n, 2], gp)
        wait(s.at[g, 0, 0, 0], recv_g.at[g, n, 1])
        ship_s(g, (col(n), (gg + 1) % 4, pl.ds(5, 5)), recv_g.at[g, n, 2], gm)

    def last_g(g, n):
        wait(s.at[g, 0, 0, 0], recv_g.at[g, n, 2])
        ship_s(g, (col(n),), recv_b.at[g, n], sib)

    def from_sibling(g):
        for n in range(4):
            wait(s.at[g, 0, 0], recv_b.at[g, n])

    def sort_w():
        for a in range(4):
            wnat[a * NK : (a + 1) * NK, :] = w_ref[a].astype(F32)
        total = jnp.zeros((160, 1280), F32)
        for n in range(5):
            row = n * 256 + lax.broadcasted_iota(jnp.int32, (256, 1280), 0)
            col = lax.broadcasted_iota(jnp.int32, (256, 1280), 1)
            perm = (row == (col & 31) * NK + (col >> 5)).astype(F32).astype(BF16)
            total += jnp.dot(wnat[:, n * 256 : (n + 1) * 256].astype(BF16), perm, preferred_element_type=F32)
        wp[...] = total.astype(BF16)

    def block(g, b):
        y1, x1, core = b // 8, b // 2 % 4, b % 2
        return (g, core) + ((y1, x1) if core else (x1, y1))

    def ladder(g, n):
        part = [s[block(g, b) + (slice(None), slice(16 * n, 16 * n + 16))] for b in range(32)]
        turned = jnp.swapaxes(jnp.concatenate(part, axis=0), 0, 1)
        for c in range(16):
            s2[:, c * 128 : (c + 1) * 128] = turned[c]
        got = jnp.dot(s2[...], v[n * 2048 : (n + 1) * 2048, :], preferred_element_type=F32)
        for a in range(4):
            if n == 0:
                lad[g, a] = got[:, a * 128 : (a + 1) * 128]
            else:
                lad[g, a] += got[:, a * 128 : (a + 1) * 128]

    def row_of(g, n):
        b, u = divmod(n, ROWS)
        return s[block(g, b) + (u,)]

    def cycle(g):
        for n in range(4):
            rows = []
            for k in range(NK):
                rows.append(jnp.concatenate([row_of(g, NM * k + 2 * n), row_of(g, NM * k + 2 * n + 1)], axis=1))
            got = jnp.dot(wp[...], jnp.concatenate(rows, axis=0), preferred_element_type=F32)
            cyc[g, n, 0] = got[:, 0:128]
            cyc[g, n, 1] = got[:, 128:256]

    def direct(g):
        for m in range(NM):
            for a in range(4):
                lad[g, a, pl.ds(m, NK, stride=NM), :] += cyc[g, m // 2, m % 2, a * NK : (a + 1) * NK, :]

    def rows_of(t):
        return pl.ds(pl.multiple_of(t * 80, 80), 80)

    def lad_of(g, t):
        return lad[g, :, rows_of(t), :].reshape(320, 128)

    def cyc_of(g, t):
        return cyc[g, t].reshape(320, 128)

    def ship(g, n, val, to):
        encode(red_out.at[g, n], val)
        send(red_out.at[g, n], red_in.at[g, n], send_r.at[g], recv_r.at[g, n], (p, to))

    def take(g, n):
        wait(red_in.at[g, n], recv_r.at[g, n])
        return decode(red_in.at[g, n])

    def cyc_1(g):
        ship(g, 2, cyc_of(g, far), down)
        ship(g, 1, cyc_of(g, up), up)

    def cyc_2(g):
        ship(g, 5, cyc_of(g, down) + take(g, 2), down)

    def lad_1(g):
        ship(g, 0, lad_of(g, far), up)
        ship(g, 3, lad_of(g, down), down)

    def lad_2(g):
        ship(g, 4, lad_of(g, up) + take(g, 0), up)

    def cyc_3(g):
        whole_cyc = (cyc_of(g, r) + take(g, 1) + take(g, 5)).reshape(2, 160, 128)
        for b in range(4):
            val = whole_cyc[:, b * NK : (b + 1) * NK, :].reshape(80, 128)
            size = jnp.maximum(jnp.max(jnp.abs(val), axis=0, keepdims=True), 1e-30)
            log = jnp.ceil(jnp.log(size) * 128.0)
            code = jnp.round(val * (jnp.exp(log * (-1 / 128)) * STEPS))
            msg[pl.ds(b, 128, stride=4), :] = jnp.concatenate([code, jnp.broadcast_to(log, (48, 128))], axis=0).T
        msg_out[g] = msg[...].astype(jnp.int32).astype(jnp.int16).reshape(32, 16, 128)
        msg_in[g, p] = msg_out[g, p]

    def lad_3(g):
        total = (lad_of(g, r) + take(g, 3) + take(g, 4)).reshape(4, 80, 128)
        for i in range(10):
            for a in range(4):
                fin[a, pl.ds(i * NK + g, NM, stride=NG), :] = total[a, i * NM : (i + 1) * NM, :]

    batches = ((0, NG - 2), (NG - 2, 2))

    def exchange(n):
        at = pl.ds(*batches[n])

        @pl.loop(1, 32)
        def _(d):
            to = (p + d) % 32
            send(msg_out.at[at, to], msg_in.at[at, p], send_m.at[n], recv_m.at[n], (to, r))

    def exchanged(n):
        part = msg_in.at[pl.ds(*batches[n]), pl.ds(0, 31)]
        wait(part, recv_m.at[n])

    def mirror(g):
        msg[...] = msg_in[g].reshape(512, 128).astype(jnp.int32).astype(F32)
        for a in range(4):
            for b in range(4):
                z[a, pl.ds(b, 32, stride=4), :] = msg[pl.ds(a * 4 + b, 32, stride=16), :]
        for a in range(4):
            turned = z[a].T
            val = turned[0:80] * (jnp.exp(turned[80:81] * (1 / 128)) * (1 / STEPS))
            for m in range(2):
                mir[a, pl.ds(pl.multiple_of((NG * m + g) * NK, 8), NK), :] = val[m * NK : (m + 1) * NK]

    start_f(0)
    start_g(0, 0)
    for g in range(1, NG):
        own(g)
    start_f(1)
    pass_f(0)
    start_g(0, 1)
    start_g(0, 2)
    last_f(0)
    start_g(0, 3)

    def step(it, _):
        done, ahead, back = it - 2, it + 1 < NG, it >= 1

        pl.when(it + 2 < NG)(lambda: start_f(it + 2))
        pl.when(ahead)(lambda: start_g(it + 1, 0))
        pass_g(it, 0)
        pl.when(it >= 2)(lambda: last_g(done, 3))

        @pl.when(ahead)
        def _():
            pass_f(it + 1)
            start_g(it + 1, 1)

        pass_g(it, 1)
        pl.when(back)(lambda: last_g(it - 1, 0))

        @pl.when(it >= 2)
        def _():
            from_sibling(done)
            cycle(done)
            cyc_1(done)

        pl.when(ahead)(lambda: start_g(it + 1, 2))
        pass_g(it, 2)
        pl.when(back)(lambda: last_g(it - 1, 1))

        @pl.when(it == 0)
        def _():
            sort_w()
            wait(v, v_sem)

        @pl.when(it >= 2)
        def _():
            ladder(done, 0)

        @pl.when(it >= 3)
        def _():
            cyc_2(it - 3)
            lad_2(it - 3)

        @pl.when(ahead)
        def _():
            last_f(it + 1)
            start_g(it + 1, 3)

        pass_g(it, 3)
        pl.when(back)(lambda: last_g(it - 1, 2))

        @pl.when(it >= 2)
        def _():
            ladder(done, 1)
            direct(done)
            lad_1(done)

        @pl.when(it >= 4)
        def _():
            cyc_3(it - 4)
            lad_3(it - 4)

        return 0

    lax.fori_loop(0, NG, step, 0)

    end = NG - 1
    last_g(end - 1, 3)
    last_g(end, 0)
    from_sibling(end - 1)
    cycle(end - 1)
    cyc_1(end - 1)
    last_g(end, 1)
    ladder(end - 1, 0)
    last_g(end, 2)
    last_g(end, 3)
    cyc_2(end - 2)
    lad_2(end - 2)
    ladder(end - 1, 1)
    direct(end - 1)
    cyc_3(end - 3)
    lad_3(end - 3)
    from_sibling(end)
    cycle(end)
    cyc_1(end)
    lad_1(end - 1)
    cyc_2(end - 1)
    ladder(end, 0)
    cyc_3(end - 2)
    exchange(0)
    ladder(end, 1)
    direct(end)
    lad_1(end)
    cyc_2(end)
    lad_2(end - 1)
    lad_3(end - 2)
    cyc_3(end - 1)
    exchanged(0)

    @pl.loop(0, NG - 2)
    def _(g):
        mirror(g)

    lad_2(end)
    cyc_3(end)
    exchange(1)
    lad_3(end - 1)
    lad_3(end)
    exchanged(1)
    mirror(end - 1)
    mirror(end)

    @pl.loop(0, 10)
    def _(i):
        rows = pl.ds(pl.multiple_of(i * NK, 8), NK)
        for a in range(4):
            lanes = slice(a * 128, (a + 1) * 128)
            residual = coul_ref[i, :, lanes].astype(F32) + fin[a, rows, :] + mir[a, rows, :]
            denom = (vir_smem[p * 4 + a] + vir_ref[...]) - occ_smem[r * 10 + i] - occ_ref[...]
            out_ref[i, :, lanes] = (residual / denom).astype(BF16)

    for g in range(NG):
        wait(s.at[g, 0], send_s.at[g])
        wait(s.at[g, 0, pl.ds(0, 3)], send_s.at[g])
        wait(s.at[g, 0, 0, pl.ds(0, 3)], send_s.at[g])
        wait(red_out.at[g], send_r.at[g])
    for n in range(2):
        wait(msg_out.at[pl.ds(*batches[n]), pl.ds(0, 31)], send_m.at[n])


def fused(amp, mask, v, w, coulomb, eps_occ, eps_vir):
    vmem = pl.BlockSpec(memory_space=pltpu.VMEM)
    smem = pl.BlockSpec(memory_space=pltpu.SMEM)
    dma = pltpu.SemaphoreType.DMA
    return pl.pallas_call(
        kernel,
        out_shape=jax.ShapeDtypeStruct((10, NK, 512), BF16),
        in_specs=[vmem, vmem, pl.BlockSpec(memory_space=pl.ANY), vmem, vmem, vmem, vmem, smem, smem],
        out_specs=vmem,
        scratch_shapes=[
            pltpu.VMEM((NG, 2, 4, 4, ROWS, NC, 128), BF16),
            pltpu.VMEM((4096, 512), BF16),
            pltpu.VMEM((160, 1280), F32),
            pltpu.VMEM((160, 1280), BF16),
            pltpu.VMEM((50 * NC, 128), F32),
            pltpu.VMEM((320, 2048), BF16),
            pltpu.VMEM((NG, 4, 320, 128), F32),
            pltpu.VMEM((NG, 4, 2, 160, 128), F32),
            pltpu.VMEM((NG, 6, 336, 128), jnp.int16),
            pltpu.VMEM((NG, 6, 336, 128), jnp.int16),
            pltpu.VMEM((512, 128), F32),
            pltpu.VMEM((4, 128, 128), F32),
            pltpu.VMEM((NG, 32, 16, 128), jnp.int16),
            pltpu.VMEM((NG, 32, 16, 128), jnp.int16),
            pltpu.VMEM((4, 400, 128), F32),
            pltpu.VMEM((4, 400, 128), F32),
            dma,
            dma((NG,)),
            dma((NG, 3)),
            dma((NG, 4, 3)),
            dma((NG, 4)),
            dma((NG,)),
            dma((NG, 6)),
            dma((2,)),
            dma((2,)),
        ],
        compiler_params=pltpu.CompilerParams(
            collective_id=0, has_side_effects=True, vmem_limit_bytes=60 * 1024 * 1024
        ),
    )(amp, mask, v, w, coulomb, eps_occ.reshape(NK, 1), eps_vir.reshape(1, 128), eps_occ, eps_vir)


def shards(amplitude, tile_mask, ladder_ints, cycle_ints, coulomb, eps_occ, eps_vir):
    pair_at = lax.axis_index("pair")
    rep_at = lax.axis_index("rep")
    rows = lax.dynamic_slice(tile_mask.reshape(1600, 2, 2), (pair_at * 50, rep_at // 2, 0), (50, 1, 2))
    mask = jnp.repeat(rows.reshape(50, 2).astype(F32), 64, axis=1)
    return fused(amplitude, mask, ladder_ints, cycle_ints, coulomb, eps_occ, eps_vir)


def solution(mesh):
    placed = (
        P("pair", "rep"),
        P(),
        P("rep", "pair"),
        P("pair", None, "rep"),
        P("rep", None, "pair"),
        P(),
        P(),
    )
    return jax.shard_map(
        shards, mesh=mesh, in_specs=placed, out_specs=P("rep", None, "pair"), check_vma=False
    )
```

```python
import jax
import jax.numpy as jnp
from jax import lax
from jax.experimental import pallas as pl
from jax.experimental.pallas import tpu as pltpu
from jax.sharding import PartitionSpec as P

NU = 10
NG = 6
NM = 4
NK = 40
STEPS = 32512.0
ROWS = 5
NC = 32
F32 = jnp.float32
BF16 = jnp.bfloat16
MESH = pl.DeviceIdType.MESH


def units(g):
    return (g + 4, 1) if isinstance(g, int) and g >= 4 else (2 * g, 2)


def encode(dst, val):
    rows = val.shape[0]
    size = jnp.maximum(jnp.max(jnp.abs(val), axis=0, keepdims=True), 1e-30)
    log = jnp.ceil(jnp.log(size) * 128.0)
    dst[0:rows] = jnp.round(val * (jnp.exp(log * (-1 / 128)) * STEPS)).astype(jnp.int32).astype(jnp.int16)
    dst[rows : rows + 16] = jnp.broadcast_to(log, (16, 128)).astype(jnp.int32).astype(jnp.int16)


def decode(src):
    rows = src.shape[0] - 16
    log = src[rows : rows + 16].astype(jnp.int32).astype(F32)[0:1]
    return src[0:rows].astype(jnp.int32).astype(F32) * (jnp.exp(log * (1 / 128)) * (1 / STEPS))


def kernel(
    amp_ref, mask_ref, v_hbm, w_ref, coul_ref, vir_ref, occ_smem, vir_smem, out_ref,
    s, v, mask, occ, wnat, wp, tmp, s2, lad, cyc, red_out, red_in, total, msg, z, msg_out, msg_in, fin, mir,
    v_sem, send_s, recv_f, recv_g, recv_b, send_r, recv_r, send_m, recv_m,
):
    p = lax.axis_index("pair")
    r = lax.axis_index("rep")
    h = p % 2
    x = (p // 2) % 4
    y = p // 8
    f = x + h * (y - x)
    gg = y + h * (x - y)
    sf = 1 + 3 * h
    sg = 4 - 3 * h

    def dev(df, dg):
        return 2 * (((f + df) % 4) * sf + ((gg + dg) % 4) * sg) + h

    sib = p + 1 - 2 * h
    fp, fm, gp, gm = dev(1, 0), dev(3, 0), dev(0, 1), dev(0, 3)
    up, down, far = (r + 1) % 4, (r + 3) % 4, (r + 2) % 4

    pltpu.make_async_copy(v_hbm, v, v_sem).start()

    barrier = pltpu.get_barrier_semaphore()

    @pl.loop(1, 32)
    def _(n):
        pl.semaphore_signal(barrier, inc=1, device_id=((p + n) % 32, r), device_id_type=MESH)

    for q in (up, down):
        pl.semaphore_signal(barrier, inc=1, device_id=(p, q), device_id_type=MESH)

    k0 = 5 * p // 4
    tile = (lax.broadcasted_iota(jnp.int32, (2, 128), 1) >= 64).astype(jnp.int32)
    spread = (lax.broadcasted_iota(jnp.int32, (2, 128), 0) == tile).astype(F32)
    for k in range(2):
        mask[k * NK : (k + 1) * NK, :] = lax.dot_general(
            mask_ref[k0 + k, r // 2].astype(F32), spread, (((0,), (0,)), ((), ())), preferred_element_type=F32
        )
    own_mask = mask[pl.ds(50 * p - 40 * k0, 50), :]

    for c in range(NC):
        piece = amp_ref[:, c * 128 : (c + 1) * 128].astype(F32) * own_mask
        tmp[pl.ds(c, 50, stride=NC), :] = piece

    def own(e):
        for u in range(ROWS):
            n = u * NU + e
            s[e, h, f, gg, u] = tmp[n * NC : (n + 1) * NC, :].astype(BF16)

    own(0)
    own(1)
    pl.semaphore_wait(barrier, 33)

    def send(src, dst, ssem, rsem, dev):
        pltpu.make_async_remote_copy(
            src_ref=src, dst_ref=dst, send_sem=ssem, recv_sem=rsem, device_id=dev, device_id_type=MESH
        ).start()

    def wait(ref, sem):
        pltpu.make_async_copy(ref, ref, sem).wait()

    def whole(g, at, sem, to):
        e, n = units(g)
        part = s.at[(pl.ds(e, n), h) + at]
        send(part, part, send_s.at[g], sem, (to, r))

    def half(g, n, at, sem, to):
        e, double = units(g)
        if double == 2:
            part = s.at[(e + n, h) + at]
        else:
            part = s.at[(e, h) + at + (pl.ds(3 * n, 3 - n),)]
        send(part, part, send_s.at[g], sem, (to, r))

    def wait_s(g, at, sem):
        wait(s.at[(pl.ds(0, units(g)[1]), 0) + at], sem)

    def start_f(g):
        whole(g, (f, gg), recv_f.at[g, 0], fp)
        whole(g, (f, gg), recv_f.at[g, 1], fm)

    def pass_f(g):
        wait_s(g, (0, 0), recv_f.at[g, 0])
        half(g, 0, ((f + 3) % 4, gg), recv_f.at[g, 2], fp)
        wait_s(g, (0, 0), recv_f.at[g, 1])
        half(g, 1, ((f + 1) % 4, gg), recv_f.at[g, 2], fm)

    def last_f(g):
        wait_s(g, (0, 0), recv_f.at[g, 2])

    def col(n):
        return (f + (0, 3, 1, 2)[n]) % 4

    def start_g(g, n):
        whole(g, (col(n), gg), recv_g.at[g, n, 0], gp)
        whole(g, (col(n), gg), recv_g.at[g, n, 1], gm)

    def pass_g(g, n):
        wait_s(g, (0, 0), recv_g.at[g, n, 0])
        half(g, 0, (col(n), (gg + 3) % 4), recv_g.at[g, n, 2], gp)
        wait_s(g, (0, 0), recv_g.at[g, n, 1])
        half(g, 1, (col(n), (gg + 1) % 4), recv_g.at[g, n, 2], gm)

    def last_g(g, n):
        wait_s(g, (0, 0), recv_g.at[g, n, 2])
        whole(g, (col(n),), recv_b.at[g, n], sib)

    def from_sibling(g):
        for n in range(4):
            wait_s(g, (0,), recv_b.at[g, n])

    def sort_w():
        for a in range(4):
            wnat[a * NK : (a + 1) * NK, :] = w_ref[a].astype(F32)
        total = jnp.zeros((160, 1280), F32)
        for n in range(5):
            row = n * 256 + lax.broadcasted_iota(jnp.int32, (256, 1280), 0)
            col = lax.broadcasted_iota(jnp.int32, (256, 1280), 1)
            perm = (row == (col & 31) * NK + (col >> 5)).astype(F32).astype(BF16)
            total += jnp.dot(wnat[:, n * 256 : (n + 1) * 256].astype(BF16), perm, preferred_element_type=F32)
        wp[...] = total.astype(BF16)

    def block(e, b):
        y1, x1, core = b // 8, b // 2 % 4, b % 2
        return (e, core) + ((y1, x1) if core else (x1, y1))

    def ladder(g, n):
        e0, double = units(g)
        part = [
            s[block(e0 + e, b) + (slice(None), slice(16 * n, 16 * n + 16))] for e in range(double) for b in range(32)
        ]
        turned = jnp.swapaxes(jnp.concatenate(part, axis=0), 0, 1)
        rows = 160 * double
        for c in range(16):
            s2[0:rows, c * 128 : (c + 1) * 128] = turned[c]
        got = jnp.dot(s2[0:rows, :], v[n * 2048 : (n + 1) * 2048, :], preferred_element_type=F32)
        for e in range(double):
            for a in range(4):
                val = got[e * 160 : (e + 1) * 160, a * 128 : (a + 1) * 128]
                if n == 0:
                    lad[e0 + e, a] = val
                else:
                    lad[e0 + e, a] += val

    def row_of(e, n):
        b, u = divmod(n, ROWS)
        return s[block(e, b) + (u,)]

    def cycle(g):
        e0, double = units(g)
        for e in range(double):
            for m in (0, 2):
                rows = [
                    jnp.concatenate([row_of(e0 + e, NM * k + m), row_of(e0 + e, NM * k + m + 1)], axis=1)
                    for k in range(NK)
                ]
                got = jnp.dot(wp[...], jnp.concatenate(rows, axis=0), preferred_element_type=F32)
                cyc[e0 + e, m] = got[:, 0:128]
                cyc[e0 + e, m + 1] = got[:, 128:256]

    def direct(g):
        e0, double = units(g)
        for e in range(double):
            for m in range(NM):
                for a in range(4):
                    lad[e0 + e, a, pl.ds(m, NK, stride=NM), :] += cyc[e0 + e, m, a * NK : (a + 1) * NK, :]

    def lad_of(g, t):
        e, n = units(g)
        return lad[pl.ds(e, n), :, pl.ds(pl.multiple_of(t * NK, 8), NK), :].reshape(160 * n, 128)

    def cyc_of(g, t):
        e, n = units(g)
        return cyc[pl.ds(e, n), t].reshape(160 * n, 128)

    def coded(buf, g, n):
        return buf.at[g, n, pl.ds(0, 160 * units(g)[1] + 16)]

    def ship(g, n, val, to):
        encode(coded(red_out, g, n), val)
        send(coded(red_out, g, n), coded(red_in, g, n), send_r.at[g], recv_r.at[g, n], (p, to))

    def take(g, n):
        wait(coded(red_in, g, n), recv_r.at[g, n])
        return decode(coded(red_in, g, n))

    def cyc_far(g):
        ship(g, 2, cyc_of(g, far), down)

    def cyc_near(g):
        ship(g, 1, cyc_of(g, up), up)

    def cyc_1(g):
        cyc_far(g)
        cyc_near(g)

    def cyc_2(g):
        ship(g, 5, cyc_of(g, down) + take(g, 2), down)

    def lad_far(g):
        ship(g, 0, lad_of(g, far), up)

    def lad_near(g):
        ship(g, 3, lad_of(g, down), down)

    def lad_1(g):
        lad_far(g)
        lad_near(g)

    def lad_2(g):
        ship(g, 4, lad_of(g, up) + take(g, 0), up)

    def cyc_3(g):
        n = units(g)[1]
        whole_cyc = (cyc_of(g, r) + take(g, 1) + take(g, 5)).reshape(n, 160, 128)
        for b in range(4):
            val = whole_cyc[:, b * NK : (b + 1) * NK, :].reshape(n * NK, 128)
            size = jnp.maximum(jnp.max(jnp.abs(val), axis=0, keepdims=True), 1e-30)
            log = jnp.ceil(jnp.log(size) * 128.0)
            code = jnp.round(val * (jnp.exp(log * (-1 / 128)) * STEPS))
            msg[pl.ds(b, 128, stride=4), :] = jnp.concatenate(
                [code, jnp.broadcast_to(log, (128 - n * NK, 128))], axis=0
            ).T
        msg_out[g] = msg[...].astype(jnp.int32).astype(jnp.int16).reshape(32, 16, 128)
        msg_in[g, p] = msg_out[g, p]

    def lad_3(g):
        e0, n = units(g)
        total[0 : 160 * n, :] = lad_of(g, r) + take(g, 3) + take(g, 4)
        for e in range(n):
            for a in range(4):
                for i in range(10):
                    at = (e * 4 + a) * NK + i * NM
                    fin[a, pl.ds(i * NK + e0 + e, NM, stride=NU), :] = total[at : at + NM, :]

    batches = ((0, 2), (2, 3), (5, 1))

    def exchange(n):
        at = pl.ds(*batches[n])

        @pl.loop(1, 32)
        def _(d):
            to = (p + d) % 32
            send(msg_out.at[at, to], msg_in.at[at, p], send_m.at[n], recv_m.at[n], (to, r))

    def exchanged(n):
        part = msg_in.at[pl.ds(*batches[n]), pl.ds(0, 31)]
        wait(part, recv_m.at[n])

    def mirror(g):
        e0, n = units(g)
        msg[...] = msg_in[g].reshape(512, 128).astype(jnp.int32).astype(F32)
        for a in range(4):
            for b in range(4):
                z[a, pl.ds(b, 32, stride=4), :] = msg[pl.ds(a * 4 + b, 32, stride=16), :]
        for a in range(4):
            turned = z[a].T
            rows = n * NK
            val = turned[0:rows] * (jnp.exp(turned[rows : rows + 1] * (1 / 128)) * (1 / STEPS))
            for e in range(n):
                mir[a, pl.ds(pl.multiple_of((e0 + e) * NK, 8), NK), :] = val[e * NK : (e + 1) * NK]

    start_f(0)
    start_g(0, 0)
    for e in range(2, NU):
        own(e)
    start_f(1)
    pass_f(0)
    start_g(0, 1)
    start_g(0, 2)
    last_f(0)
    start_g(0, 3)

    def step(it, _):
        done, ahead, back, small = it - 2, it < 3, it >= 1, it == 3

        pl.when(it < 2)(lambda: start_f(it + 2))
        pl.when(it == 2)(lambda: start_f(4))
        pl.when(small)(lambda: start_f(5))
        pl.when(ahead)(lambda: start_g(it + 1, 0))
        pl.when(small)(lambda: start_g(4, 0))
        pass_g(it, 0)
        pl.when(it >= 2)(lambda: last_g(done, 3))

        @pl.when(ahead)
        def _():
            pass_f(it + 1)
            start_g(it + 1, 1)

        @pl.when(small)
        def _():
            pass_f(4)
            start_g(4, 1)

        pass_g(it, 1)
        pl.when(back)(lambda: last_g(it - 1, 0))

        @pl.when(it >= 2)
        def _():
            from_sibling(done)
            cycle(done)
            cyc_1(done)

        pl.when(ahead)(lambda: start_g(it + 1, 2))
        pl.when(small)(lambda: start_g(4, 2))
        pass_g(it, 2)
        pl.when(back)(lambda: last_g(it - 1, 1))

        @pl.when(it == 0)
        def _():
            sort_w()
            for j in range(NK):
                occ[j : j + 1, :] = jnp.full((1, 128), occ_smem[j], F32)
            wait(v, v_sem)

        pl.when(it >= 2)(lambda: ladder(done, 0))

        @pl.when(it >= 3)
        def _():
            cyc_2(it - 3)
            lad_2(it - 3)

        @pl.when(ahead)
        def _():
            last_f(it + 1)
            start_g(it + 1, 3)

        @pl.when(small)
        def _():
            last_f(4)
            start_g(4, 3)

        pass_g(it, 3)
        pl.when(back)(lambda: last_g(it - 1, 2))

        @pl.when(it >= 2)
        def _():
            ladder(done, 1)
            direct(done)
            lad_1(done)

        return 0

    lax.fori_loop(0, 4, step, 0)

    start_g(5, 0)
    pass_g(4, 0)
    last_g(2, 3)
    pass_f(5)
    start_g(5, 1)
    pass_g(4, 1)
    last_g(3, 0)
    from_sibling(2)
    cycle(2)
    cyc_1(2)
    start_g(5, 2)
    pass_g(4, 2)
    last_g(3, 1)
    last_f(5)
    start_g(5, 3)
    pass_g(4, 3)
    last_g(3, 2)
    ladder(2, 0)
    pass_g(5, 0)
    last_g(3, 3)
    cyc_2(1)
    lad_2(1)
    ladder(2, 1)
    direct(2)
    lad_1(2)
    pass_g(5, 1)
    last_g(4, 0)
    cyc_3(0)
    lad_3(0)
    from_sibling(3)
    cycle(3)
    cyc_1(3)
    pass_g(5, 2)
    last_g(4, 1)
    pass_g(5, 3)
    last_g(4, 2)
    ladder(3, 0)
    last_g(4, 3)
    last_g(5, 0)
    cyc_2(2)
    ladder(3, 1)
    direct(3)
    lad_1(3)
    last_g(5, 1)
    last_g(5, 2)
    last_g(5, 3)
    lad_2(2)
    from_sibling(4)
    cycle(4)
    cyc_far(4)
    from_sibling(5)
    cycle(5)
    cyc_far(5)
    cyc_2(3)
    cyc_near(4)
    cyc_3(1)
    exchange(0)
    ladder(4, 0)
    ladder(4, 1)
    direct(4)
    lad_1(4)
    lad_2(3)
    cyc_2(4)
    cyc_2(5)
    ladder(5, 0)
    ladder(5, 1)
    direct(5)
    lad_far(5)
    cyc_near(5)
    lad_near(5)
    cyc_3(2)
    lad_3(1)
    lad_2(4)
    cyc_3(3)
    cyc_3(4)
    exchange(1)
    lad_2(5)
    cyc_3(5)
    exchange(2)
    lad_3(2)
    lad_3(3)
    exchanged(0)
    mirror(0)
    mirror(1)
    lad_3(4)
    exchanged(1)
    for g in (2, 3, 4):
        mirror(g)
    lad_3(5)
    exchanged(2)
    mirror(5)

    @pl.loop(0, 10)
    def _(i):
        rows = pl.ds(pl.multiple_of(i * NK, 8), NK)
        for a in range(4):
            lanes = slice(a * 128, (a + 1) * 128)
            residual = coul_ref[i, :, lanes].astype(F32) + fin[a, rows, :] + mir[a, rows, :]
            denom = (vir_smem[p * 4 + a] + vir_ref[...]) - occ_smem[r * 10 + i] - occ[...]
            out_ref[i, :, lanes] = (residual / denom).astype(BF16)

    for g in range(NG):
        wait_s(g, (), send_s.at[g])
        wait_s(g, (pl.ds(0, 3),), send_s.at[g])
        wait_s(g, (0, pl.ds(0, 3)), send_s.at[g])
        wait(red_out.at[g, :, pl.ds(0, 160 * units(g)[1] + 16)], send_r.at[g])
    for n in range(3):
        wait(msg_out.at[pl.ds(*batches[n]), pl.ds(0, 31)], send_m.at[n])


def fused(amp, mask, v, w, coulomb, eps_occ, eps_vir):
    vmem = pl.BlockSpec(memory_space=pltpu.VMEM)
    smem = pl.BlockSpec(memory_space=pltpu.SMEM)
    dma = pltpu.SemaphoreType.DMA
    return pl.pallas_call(
        kernel,
        out_shape=jax.ShapeDtypeStruct((10, NK, 512), BF16),
        in_specs=[vmem, vmem, pl.BlockSpec(memory_space=pl.ANY), vmem, vmem, vmem, smem, smem],
        out_specs=vmem,
        scratch_shapes=[
            pltpu.VMEM((NU, 2, 4, 4, ROWS, NC, 128), BF16),
            pltpu.VMEM((4096, 512), BF16),
            pltpu.VMEM((80, 128), F32),
            pltpu.VMEM((NK, 128), F32),
            pltpu.VMEM((160, 1280), F32),
            pltpu.VMEM((160, 1280), BF16),
            pltpu.VMEM((50 * NC, 128), F32),
            pltpu.VMEM((320, 2048), BF16),
            pltpu.VMEM((NU, 4, 160, 128), F32),
            pltpu.VMEM((NU, 4, 160, 128), F32),
            pltpu.VMEM((NG, 6, 336, 128), jnp.int16),
            pltpu.VMEM((NG, 6, 336, 128), jnp.int16),
            pltpu.VMEM((320, 128), F32),
            pltpu.VMEM((512, 128), F32),
            pltpu.VMEM((4, 128, 128), F32),
            pltpu.VMEM((NG, 32, 16, 128), jnp.int16),
            pltpu.VMEM((NG, 32, 16, 128), jnp.int16),
            pltpu.VMEM((4, 400, 128), F32),
            pltpu.VMEM((4, 400, 128), F32),
            dma,
            dma((NG,)),
            dma((NG, 3)),
            dma((NG, 4, 3)),
            dma((NG, 4)),
            dma((NG,)),
            dma((NG, 6)),
            dma((3,)),
            dma((3,)),
        ],
        compiler_params=pltpu.CompilerParams(
            collective_id=0, has_side_effects=True, vmem_limit_bytes=60 * 1024 * 1024
        ),
    )(amp, mask, v, w, coulomb, eps_vir.reshape(1, 128), eps_occ, eps_vir)


def shards(amplitude, tile_mask, ladder_ints, cycle_ints, coulomb, eps_occ, eps_vir):
    mask = jnp.transpose(tile_mask, (0, 2, 3, 1))
    return fused(amplitude, mask, ladder_ints, cycle_ints, coulomb, eps_occ, eps_vir)


def solution(mesh):
    placed = (
        P("pair", "rep"),
        P(),
        P("rep", "pair"),
        P("pair", None, "rep"),
        P("rep", None, "pair"),
        P(),
        P(),
    )
    return jax.shard_map(
        shards, mesh=mesh, in_specs=placed, out_specs=P("rep", None, "pair"), check_vma=False
    )
```

```python
import jax
import jax.numpy as jnp
from jax import lax
from jax.experimental import pallas as pl
from jax.experimental.pallas import tpu as pltpu
from jax.sharding import PartitionSpec as P

NU = 10
NG = 6
NM = 4
NK = 40
STEPS = 32512.0
ROWS = 5
NC = 32
F32 = jnp.float32
BF16 = jnp.bfloat16
MESH = pl.DeviceIdType.MESH


def units(g):
    return (g + 4, 1) if isinstance(g, int) and g >= 4 else (2 * g, 2)


def encode(dst, val):
    rows = val.shape[0]
    size = jnp.maximum(jnp.max(jnp.abs(val), axis=0, keepdims=True), 1e-30)
    log = jnp.ceil(jnp.log(size) * 128.0)
    dst[0:rows] = jnp.round(val * (jnp.exp(log * (-1 / 128)) * STEPS)).astype(jnp.int32).astype(jnp.int16)
    dst[rows : rows + 16] = jnp.broadcast_to(log, (16, 128)).astype(jnp.int32).astype(jnp.int16)


def decode(src):
    rows = src.shape[0] - 16
    log = src[rows : rows + 16].astype(jnp.int32).astype(F32)[0:1]
    return src[0:rows].astype(jnp.int32).astype(F32) * (jnp.exp(log * (1 / 128)) * (1 / STEPS))


def kernel(
    amp_ref, mask_ref, v_hbm, w_hbm, coul_hbm, vir_ref, occ_smem, vir_smem, out_ref,
    s, v, w_ref, coul_ref, mask, occ, wnat, wp, tmp, s2, lad, cyc, red_out, red_in, total, msg, z, msg_out, msg_in, fin, mir,
    v_sem, w_sem, coul_sem, send_s, recv_f, recv_g, recv_b, send_r, recv_r, send_m, recv_m,
):
    p = lax.axis_index("pair")
    r = lax.axis_index("rep")
    h = p % 2
    x = (p // 2) % 4
    y = p // 8
    f = x + h * (y - x)
    gg = y + h * (x - y)
    sf = 1 + 3 * h
    sg = 4 - 3 * h

    def dev(df, dg):
        return 2 * (((f + df) % 4) * sf + ((gg + dg) % 4) * sg) + h

    sib = p + 1 - 2 * h
    fp, fm, gp, gm = dev(1, 0), dev(3, 0), dev(0, 1), dev(0, 3)
    up, down, far = (r + 1) % 4, (r + 3) % 4, (r + 2) % 4

    pltpu.make_async_copy(w_hbm, w_ref, w_sem).start()
    pltpu.make_async_copy(v_hbm, v, v_sem).start()
    pltpu.make_async_copy(coul_hbm, coul_ref, coul_sem).start()

    barrier = pltpu.get_barrier_semaphore()

    @pl.loop(1, 32)
    def _(n):
        pl.semaphore_signal(barrier, inc=1, device_id=((p + n) % 32, r), device_id_type=MESH)

    for q in (up, down):
        pl.semaphore_signal(barrier, inc=1, device_id=(p, q), device_id_type=MESH)

    k0 = 5 * p // 4
    tile = (lax.broadcasted_iota(jnp.int32, (2, 128), 1) >= 64).astype(jnp.int32)
    spread = (lax.broadcasted_iota(jnp.int32, (2, 128), 0) == tile).astype(F32)
    for k in range(2):
        mask[k * NK : (k + 1) * NK, :] = lax.dot_general(
            mask_ref[k0 + k, r // 2].astype(F32), spread, (((0,), (0,)), ((), ())), preferred_element_type=F32
        )
    own_mask = mask[pl.ds(50 * p - 40 * k0, 50), :]

    for c in range(NC):
        piece = amp_ref[:, c * 128 : (c + 1) * 128].astype(F32) * own_mask
        tmp[pl.ds(c, 50, stride=NC), :] = piece

    def own(e):
        for u in range(ROWS):
            n = u * NU + e
            s[e, h, f, gg, u] = tmp[n * NC : (n + 1) * NC, :].astype(BF16)

    own(0)
    own(1)
    pl.semaphore_wait(barrier, 33)

    def send(src, dst, ssem, rsem, dev):
        pltpu.make_async_remote_copy(
            src_ref=src, dst_ref=dst, send_sem=ssem, recv_sem=rsem, device_id=dev, device_id_type=MESH
        ).start()

    def wait(ref, sem):
        pltpu.make_async_copy(ref, ref, sem).wait()

    def whole(g, at, sem, to):
        e, n = units(g)
        part = s.at[(pl.ds(e, n), h) + at]
        send(part, part, send_s.at[g], sem, (to, r))

    def half(g, n, at, sem, to):
        e, double = units(g)
        if double == 2:
            part = s.at[(e + n, h) + at]
        else:
            part = s.at[(e, h) + at + (pl.ds(3 * n, 3 - n),)]
        send(part, part, send_s.at[g], sem, (to, r))

    def wait_s(g, at, sem):
        wait(s.at[(pl.ds(0, units(g)[1]), 0) + at], sem)

    def start_f(g):
        whole(g, (f, gg), recv_f.at[g, 0], fp)
        whole(g, (f, gg), recv_f.at[g, 1], fm)

    def pass_f(g):
        wait_s(g, (0, 0), recv_f.at[g, 0])
        half(g, 0, ((f + 3) % 4, gg), recv_f.at[g, 2], fp)
        wait_s(g, (0, 0), recv_f.at[g, 1])
        half(g, 1, ((f + 1) % 4, gg), recv_f.at[g, 2], fm)

    def last_f(g):
        wait_s(g, (0, 0), recv_f.at[g, 2])

    def col(n):
        return (f + (0, 3, 1, 2)[n]) % 4

    def start_g(g, n):
        whole(g, (col(n), gg), recv_g.at[g, n, 0], gp)
        whole(g, (col(n), gg), recv_g.at[g, n, 1], gm)

    def pass_g(g, n):
        wait_s(g, (0, 0), recv_g.at[g, n, 0])
        half(g, 0, (col(n), (gg + 3) % 4), recv_g.at[g, n, 2], gp)
        wait_s(g, (0, 0), recv_g.at[g, n, 1])
        half(g, 1, (col(n), (gg + 1) % 4), recv_g.at[g, n, 2], gm)

    def last_g(g, n):
        wait_s(g, (0, 0), recv_g.at[g, n, 2])
        whole(g, (col(n),), recv_b.at[g, n], sib)

    def from_sibling(g):
        for n in range(4):
            wait_s(g, (0,), recv_b.at[g, n])

    def sort_w():
        for a in range(4):
            wnat[a * NK : (a + 1) * NK, :] = w_ref[a].astype(F32)
        total = jnp.zeros((160, 1280), F32)
        for n in range(5):
            row = n * 256 + lax.broadcasted_iota(jnp.int32, (256, 1280), 0)
            col = lax.broadcasted_iota(jnp.int32, (256, 1280), 1)
            perm = (row == (col & 31) * NK + (col >> 5)).astype(F32).astype(BF16)
            total += jnp.dot(wnat[:, n * 256 : (n + 1) * 256].astype(BF16), perm, preferred_element_type=F32)
        wp[...] = total.astype(BF16)

    def block(e, b):
        y1, x1, core = b // 8, b // 2 % 4, b % 2
        return (e, core) + ((y1, x1) if core else (x1, y1))

    def ladder(g, n):
        e0, double = units(g)
        part = [
            s[block(e0 + e, b) + (slice(None), slice(16 * n, 16 * n + 16))] for e in range(double) for b in range(32)
        ]
        turned = jnp.swapaxes(jnp.concatenate(part, axis=0), 0, 1)
        rows = 160 * double
        for c in range(16):
            s2[0:rows, c * 128 : (c + 1) * 128] = turned[c]
        got = jnp.dot(s2[0:rows, :], v[n * 2048 : (n + 1) * 2048, :], preferred_element_type=F32)
        for e in range(double):
            for a in range(4):
                val = got[e * 160 : (e + 1) * 160, a * 128 : (a + 1) * 128]
                if n == 0:
                    lad[e0 + e, a] = val
                else:
                    lad[e0 + e, a] += val

    def row_of(e, n):
        b, u = divmod(n, ROWS)
        return s[block(e, b) + (u,)]

    def cycle(g):
        e0, double = units(g)
        for e in range(double):
            for m in (0, 2):
                rows = [
                    jnp.concatenate([row_of(e0 + e, NM * k + m), row_of(e0 + e, NM * k + m + 1)], axis=1)
                    for k in range(NK)
                ]
                got = jnp.dot(wp[...], jnp.concatenate(rows, axis=0), preferred_element_type=F32)
                cyc[e0 + e, m] = got[:, 0:128]
                cyc[e0 + e, m + 1] = got[:, 128:256]

    def direct(g):
        e0, double = units(g)
        for e in range(double):
            for m in range(NM):
                for a in range(4):
                    lad[e0 + e, a, pl.ds(m, NK, stride=NM), :] += cyc[e0 + e, m, a * NK : (a + 1) * NK, :]

    def lad_of(g, t):
        e, n = units(g)
        return lad[pl.ds(e, n), :, pl.ds(pl.multiple_of(t * NK, 8), NK), :].reshape(160 * n, 128)

    def cyc_of(g, t):
        e, n = units(g)
        return cyc[pl.ds(e, n), t].reshape(160 * n, 128)

    def coded(buf, g, n):
        return buf.at[g, n, pl.ds(0, 160 * units(g)[1] + 16)]

    def ship(g, n, val, to):
        encode(coded(red_out, g, n), val)
        send(coded(red_out, g, n), coded(red_in, g, n), send_r.at[g], recv_r.at[g, n], (p, to))

    def take(g, n):
        wait(coded(red_in, g, n), recv_r.at[g, n])
        return decode(coded(red_in, g, n))

    def cyc_far(g):
        ship(g, 2, cyc_of(g, far), down)

    def cyc_near(g):
        ship(g, 1, cyc_of(g, up), up)

    def cyc_1(g):
        cyc_far(g)
        cyc_near(g)

    def cyc_2(g):
        ship(g, 5, cyc_of(g, down) + take(g, 2), down)

    def lad_far(g):
        ship(g, 0, lad_of(g, far), up)

    def lad_near(g):
        ship(g, 3, lad_of(g, down), down)

    def lad_1(g):
        lad_far(g)
        lad_near(g)

    def lad_2(g):
        ship(g, 4, lad_of(g, up) + take(g, 0), up)

    def cyc_3(g):
        n = 2
        if isinstance(g, int) and g == 4:
            parts = [cyc_of(k, r) + take(k, 1) + take(k, 5) for k in (4, 5)]
            whole_cyc = jnp.concatenate(parts, axis=0).reshape(n, 160, 128)
        else:
            whole_cyc = (cyc_of(g, r) + take(g, 1) + take(g, 5)).reshape(n, 160, 128)
        for b in range(4):
            val = whole_cyc[:, b * NK : (b + 1) * NK, :].reshape(n * NK, 128)
            size = jnp.maximum(jnp.max(jnp.abs(val), axis=0, keepdims=True), 1e-30)
            log = jnp.ceil(jnp.log(size) * 128.0)
            code = jnp.round(val * (jnp.exp(log * (-1 / 128)) * STEPS))
            msg[pl.ds(b, 128, stride=4), :] = jnp.concatenate(
                [code, jnp.broadcast_to(log, (128 - n * NK, 128))], axis=0
            ).T
        msg_out[g] = msg[...].astype(jnp.int32).astype(jnp.int16).reshape(32, 16, 128)
        msg_in[g, p] = msg_out[g, p]

    def lad_3(g):
        e0, n = units(g)
        total[0 : 160 * n, :] = lad_of(g, r) + take(g, 3) + take(g, 4)
        for e in range(n):
            for a in range(4):
                for i in range(10):
                    at = (e * 4 + a) * NK + i * NM
                    fin[a, pl.ds(i * NK + e0 + e, NM, stride=NU), :] = total[at : at + NM, :]

    batches = ((0, 2), (2, 2), (4, 1))

    def exchange(n):
        at = pl.ds(*batches[n])

        @pl.loop(1, 32)
        def _(d):
            to = (p + d) % 32
            send(msg_out.at[at, to], msg_in.at[at, p], send_m.at[n], recv_m.at[n], (to, r))

    def exchanged(n):
        part = msg_in.at[pl.ds(*batches[n]), pl.ds(0, 31)]
        wait(part, recv_m.at[n])

    def mirror(g):
        e0, n = 2 * g, 2
        msg[...] = msg_in[g].reshape(512, 128).astype(jnp.int32).astype(F32)
        for a in range(4):
            for b in range(4):
                z[a, pl.ds(b, 32, stride=4), :] = msg[pl.ds(a * 4 + b, 32, stride=16), :]
        for a in range(4):
            turned = z[a].T
            rows = n * NK
            val = turned[0:rows] * (jnp.exp(turned[rows : rows + 1] * (1 / 128)) * (1 / STEPS))
            for e in range(n):
                mir[a, pl.ds(pl.multiple_of((e0 + e) * NK, 8), NK), :] = val[e * NK : (e + 1) * NK]

    start_f(0)
    start_g(0, 0)
    for e in range(2, NU):
        own(e)
    start_f(1)
    start_g(1, 0)
    pass_f(0)
    start_g(0, 1)
    start_g(0, 2)
    last_f(0)
    start_g(0, 3)

    def step(it, _):
        done, ahead, back, small = it - 2, it < 3, it >= 1, it == 3

        def start(g):
            start_f(g)
            start_g(g, 0)

        pl.when(it < 2)(lambda: start(it + 2))
        pl.when(it == 2)(lambda: start(4))
        pl.when(small)(lambda: start(5))
        pass_g(it, 0)
        pl.when(it >= 2)(lambda: last_g(done, 3))

        @pl.when(ahead)
        def _():
            pass_f(it + 1)
            start_g(it + 1, 1)

        @pl.when(small)
        def _():
            pass_f(4)
            start_g(4, 1)

        pass_g(it, 1)
        pl.when(back)(lambda: last_g(it - 1, 0))

        @pl.when(it >= 2)
        def _():
            from_sibling(done)
            cycle(done)
            cyc_1(done)

        pl.when(ahead)(lambda: start_g(it + 1, 2))
        pl.when(small)(lambda: start_g(4, 2))
        pass_g(it, 2)
        pl.when(back)(lambda: last_g(it - 1, 1))

        @pl.when(it == 0)
        def _():
            wait(w_ref, w_sem)
            sort_w()
            for j in range(NK):
                occ[j : j + 1, :] = jnp.full((1, 128), occ_smem[j], F32)
            wait(v, v_sem)
            wait(coul_ref, coul_sem)

        pl.when(it >= 2)(lambda: ladder(done, 0))

        @pl.when(it >= 3)
        def _():
            cyc_2(it - 3)
            lad_2(it - 3)

        @pl.when(ahead)
        def _():
            last_f(it + 1)
            start_g(it + 1, 3)

        @pl.when(small)
        def _():
            last_f(4)
            start_g(4, 3)

        pass_g(it, 3)
        pl.when(back)(lambda: last_g(it - 1, 2))

        @pl.when(it >= 2)
        def _():
            ladder(done, 1)
            direct(done)
            lad_1(done)

        return 0

    lax.fori_loop(0, 4, step, 0)

    pass_g(4, 0)
    last_g(2, 3)
    pass_f(5)
    start_g(5, 1)
    pass_g(4, 1)
    last_g(3, 0)
    from_sibling(2)
    cycle(2)
    cyc_1(2)
    start_g(5, 2)
    pass_g(4, 2)
    last_g(3, 1)
    last_f(5)
    start_g(5, 3)
    pass_g(4, 3)
    last_g(3, 2)
    ladder(2, 0)
    pass_g(5, 0)
    last_g(3, 3)
    cyc_2(1)
    lad_2(1)
    ladder(2, 1)
    direct(2)
    lad_1(2)
    pass_g(5, 1)
    last_g(4, 0)
    cyc_3(0)
    lad_3(0)
    from_sibling(3)
    cycle(3)
    cyc_1(3)
    pass_g(5, 2)
    last_g(4, 1)
    pass_g(5, 3)
    last_g(4, 2)
    ladder(3, 0)
    last_g(4, 3)
    last_g(5, 0)
    cyc_2(2)
    ladder(3, 1)
    direct(3)
    lad_1(3)
    last_g(5, 1)
    last_g(5, 2)
    last_g(5, 3)
    lad_2(2)
    from_sibling(4)
    cycle(4)
    cyc_far(4)
    from_sibling(5)
    cycle(5)
    cyc_far(5)
    cyc_2(3)
    cyc_near(4)
    cyc_3(1)
    exchange(0)
    ladder(4, 0)
    ladder(4, 1)
    direct(4)
    lad_1(4)
    lad_2(3)
    cyc_2(4)
    cyc_2(5)
    ladder(5, 0)
    ladder(5, 1)
    direct(5)
    lad_far(5)
    cyc_near(5)
    lad_near(5)
    cyc_3(2)
    lad_3(1)
    lad_2(4)
    cyc_3(3)
    exchange(1)
    lad_2(5)
    cyc_3(4)
    exchange(2)
    lad_3(2)
    lad_3(3)
    exchanged(0)
    mirror(0)
    mirror(1)
    lad_3(4)
    exchanged(1)
    mirror(2)
    mirror(3)
    lad_3(5)
    exchanged(2)
    mirror(4)

    @pl.loop(0, 10)
    def _(i):
        rows = pl.ds(pl.multiple_of(i * NK, 8), NK)
        for a in range(4):
            lanes = slice(a * 128, (a + 1) * 128)
            residual = coul_ref[i, :, lanes].astype(F32) + fin[a, rows, :] + mir[a, rows, :]
            denom = (vir_smem[p * 4 + a] + vir_ref[...]) - occ_smem[r * 10 + i] - occ[...]
            out_ref[i, :, lanes] = (residual / denom).astype(BF16)

    for g in range(NG):
        wait_s(g, (), send_s.at[g])
        wait_s(g, (pl.ds(0, 3),), send_s.at[g])
        wait_s(g, (0, pl.ds(0, 3)), send_s.at[g])
        wait(red_out.at[g, :, pl.ds(0, 160 * units(g)[1] + 16)], send_r.at[g])
    for n in range(3):
        wait(msg_out.at[pl.ds(*batches[n]), pl.ds(0, 31)], send_m.at[n])


def fused(amp, mask, v, w, coulomb, eps_occ, eps_vir):
    vmem = pl.BlockSpec(memory_space=pltpu.VMEM)
    smem = pl.BlockSpec(memory_space=pltpu.SMEM)
    dma = pltpu.SemaphoreType.DMA
    return pl.pallas_call(
        kernel,
        out_shape=jax.ShapeDtypeStruct((10, NK, 512), BF16),
        in_specs=[vmem, vmem] + [pl.BlockSpec(memory_space=pl.ANY)] * 3 + [vmem, smem, smem],
        out_specs=vmem,
        scratch_shapes=[
            pltpu.VMEM((NU, 2, 4, 4, ROWS, NC, 128), BF16),
            pltpu.VMEM((4096, 512), BF16),
            pltpu.VMEM((4, NK, 1280), BF16),
            pltpu.VMEM((10, NK, 512), BF16),
            pltpu.VMEM((80, 128), F32),
            pltpu.VMEM((NK, 128), F32),
            pltpu.VMEM((160, 1280), F32),
            pltpu.VMEM((160, 1280), BF16),
            pltpu.VMEM((50 * NC, 128), F32),
            pltpu.VMEM((320, 2048), BF16),
            pltpu.VMEM((NU, 4, 160, 128), F32),
            pltpu.VMEM((NU, 4, 160, 128), F32),
            pltpu.VMEM((NG, 6, 336, 128), jnp.int16),
            pltpu.VMEM((NG, 6, 336, 128), jnp.int16),
            pltpu.VMEM((320, 128), F32),
            pltpu.VMEM((512, 128), F32),
            pltpu.VMEM((4, 128, 128), F32),
            pltpu.VMEM((5, 32, 16, 128), jnp.int16),
            pltpu.VMEM((5, 32, 16, 128), jnp.int16),
            pltpu.VMEM((4, 400, 128), F32),
            pltpu.VMEM((4, 400, 128), F32),
            dma,
            dma,
            dma,
            dma((NG,)),
            dma((NG, 3)),
            dma((NG, 4, 3)),
            dma((NG, 4)),
            dma((NG,)),
            dma((NG, 6)),
            dma((3,)),
            dma((3,)),
        ],
        compiler_params=pltpu.CompilerParams(
            collective_id=0, has_side_effects=True, vmem_limit_bytes=60 * 1024 * 1024
        ),
    )(amp, mask, v, w, coulomb, eps_vir.reshape(1, 128), eps_occ, eps_vir)


def shards(amplitude, tile_mask, ladder_ints, cycle_ints, coulomb, eps_occ, eps_vir):
    mask = jnp.transpose(tile_mask, (0, 2, 3, 1))
    return fused(amplitude, mask, ladder_ints, cycle_ints, coulomb, eps_occ, eps_vir)


def solution(mesh):
    placed = (
        P("pair", "rep"),
        P(),
        P("rep", "pair"),
        P("pair", None, "rep"),
        P("rep", None, "pair"),
        P(),
        P(),
    )
    return jax.shard_map(
        shards, mesh=mesh, in_specs=placed, out_specs=P("rep", None, "pair"), check_vma=False
    )
```
